128 devices in a mesh: chan: 8 (over y, core), tile: 16 (over x, z).
Axes of the slice: x: 4, y: 4, z: 4, core: 2. Of those that a mesh axis runs over, the one named last changes fastest.
Arguments:
- sky_cube: float32 [256, 512, 1024], P('chan', 'tile'), may hold values from -8 to 8
- pixel_mask: int32 [512, 1024], P('tile'), may hold values 0 or 1
- radius: int32 [256], replicated, may hold values from 1 to 4, as said below
- chan_weight: float32 [256], replicated, may hold values from 0.5 to 2
- band: float32 [17, 256], replicated, may hold values from -0.15 to 0.15
- resample: float32 [256, 256], replicated, may hold values from -0.375 to 0.375
- slab_index: int32 [256], replicated, may hold values from 0 to 15, never falling along the last dimension, each value on 1 to 20 neighbouring positions
Outputs:
- slabs: float32 [320, 512, 1024], P('tile', None, 'chan')
The draws below stay inside these ranges and needn't reach their ends.
Inputs may be any that keep to these rules, and one draw needn't show every extreme that they name: Every channel's radius is 1 to 4; some channel has 4. `slab_index`: never falls along the rows; each owner gets 1 to 20 rows and some owner exactly 20.
All inputs are finite; a program needn't handle non-finite values. No bound on the sum of `pixel_mask` on one device may be relied on, other than what follows from the above.
Results may differ from the reference program's by a relative error of at most 0.00007.
Values sent between devices are 32-bit elements; how exact they have to be, the bound alone decides.
A program may use at most 128 MiB of HBM per device.

```python
import math
import jax
import jax.numpy as jnp
import numpy as np
from jax import lax

NCH = 256
PCOLS = 1024
NOUT = 256
CAP = 20
RMAX = 4
BW = 8
PROWS = 512
N_TILE = 16


def draw_radius(key, part):
    values = jax.random.randint(key, (NCH,), 1, RMAX + 1)
    chosen = jax.random.randint(jax.random.fold_in(key, 7), (), 0, NCH)
    return jnp.where(jnp.arange(NCH) == chosen, RMAX, values).astype(jnp.int32)


def plant(array, stream_key, low, largest):
    place = [jax.random.randint(jax.random.fold_in(stream_key, axis), (), 0, length) for axis, length in enumerate(array.shape)]
    main_axis = array.shape.index(max(array.shape))
    next_to = place[:main_axis] + [(place[main_axis] + 1) % array.shape[main_axis]] + place[main_axis + 1:]
    return array.at[tuple(place)].set(low).at[tuple(next_to)].set(largest)


def shard_levels(own_key, extent, shards, smallest, high):
    level = 1.0
    for axis_at, parts in shards:
        draws = jax.random.uniform(jax.random.fold_in(jax.random.fold_in(own_key, 6), axis_at), (parts,), jnp.float32, smallest / len(shards), high / len(shards))
        level = level * jnp.repeat(jnp.exp(draws), extent[axis_at] // parts).reshape((-1,) + (1,) * (len(extent) - 1 - axis_at))
    return level


def profile(amount, total, reach, lean):
    loads = [(1 << 20) // math.isqrt(grade ** lean) + 1 for grade in range(2, amount + 1)]
    spare, holding = total - reach - (amount - 1), [1] * (amount - 1)
    while spare > 0:
        free = [i for i in range(amount - 1) if holding[i] < reach]
        whole, remaining = sum([loads[i] for i in free]), spare
        for i in free:
            addition = min(reach - holding[i], max(1, remaining * loads[i] // whole), spare)
            holding[i] = holding[i] + addition
            spare = spare - addition
    return np.array([reach] + holding)


def ragged_sizes(stream_key, amount, total, reach, skew):
    if amount == 2:
        one = jax.random.randint(stream_key, (), max(1, total - reach), min(reach, total - 1) + 1)
        return jnp.stack([one, total - one])
    tallies = jnp.asarray(profile(amount, total, reach, skew), jnp.int32)
    couples = (amount - 1) // 2
    donor, receiver = tallies[1:1 + 2 * couples:2], tallies[2:2 + 2 * couples:2]
    slack = jnp.minimum(donor - 1, reach - receiver)
    moved = jax.random.randint(jax.random.fold_in(stream_key, 1), (couples,), 0, 1 << 20) % (slack + 1)
    tallies = tallies.at[1:1 + 2 * couples:2].set(donor - moved).at[2:2 + 2 * couples:2].set(receiver + moved)
    return tallies[jax.random.permutation(jax.random.fold_in(stream_key, 2), amount)]


def noise(stream_key, extent, scale, limit, cuts=(), kind=jnp.bfloat16):
    level = shard_levels(stream_key, extent, cuts, -0.22, 0.18) if cuts else 1.0
    drawn = jax.random.normal(stream_key, extent, jnp.float32) * scale * level
    return jnp.minimum(jnp.maximum(drawn, -limit), limit).astype(kind)


def setup_inputs(seed: int = 0) -> dict:
    key_of = jax.random.split(jax.random.key(seed), 8)
    return {
        "sky_cube": noise(key_of[0], (NCH, PROWS, PCOLS), 1.0, 8.0, ((0, 8), (1, 16)), jnp.float32),
        "pixel_mask": plant((jax.random.randint(key_of[1], (PROWS, PCOLS), 0, 10) < 9).astype(jnp.int32), jax.random.fold_in(key_of[1], 1), 0, 1),
        "radius": draw_radius(jax.random.fold_in(key_of[7], 71), 0),
        "chan_weight": jnp.clip(jnp.exp(jax.random.uniform(key_of[3], (NCH,), jnp.float32, math.log(0.5), math.log(2.0))), 0.5, 2.0),
        "band": jnp.clip(jax.random.uniform(key_of[4], (2 * BW + 1, NCH), jnp.float32, -0.15, 0.15), -0.15, 0.15),
        "resample": noise(key_of[5], (NOUT, NCH), NCH ** -0.5, 0.375, (), jnp.float32),
        "slab_index": jnp.searchsorted(jnp.cumsum(ragged_sizes(key_of[6], N_TILE, NOUT, CAP, 2)), jnp.arange(NOUT), side="right").astype(jnp.int32),
    }


def make_taps(radius):
    spread = radius.astype(jnp.float32)[:, None]
    offsets = jnp.arange(-RMAX, RMAX + 1).astype(jnp.float32)[None, :]
    sigma = 0.5 * spread + 0.5
    values = jnp.exp(-offsets * offsets / (2.0 * sigma * sigma))
    values = jnp.where(jnp.abs(offsets) <= spread, values, jnp.zeros_like(values))
    return values / jnp.sum(values, axis=1, keepdims=True)


def reference(sky_cube, pixel_mask, radius, chan_weight, band, resample, slab_index):
    taps = make_taps(radius)
    masked = sky_cube * pixel_mask.astype(sky_cube.dtype)[None]
    padded = jnp.pad(masked, ((0, 0), (RMAX, RMAX), (0, 0)))
    along_rows = jnp.zeros_like(masked)
    for offset in range(2 * RMAX + 1):
        along_rows = along_rows + taps[:, offset, None, None] * padded[:, offset:offset + PROWS, :]
    padded = jnp.pad(along_rows, ((0, 0), (0, 0), (RMAX, RMAX)))
    beam = jnp.zeros_like(masked)
    for offset in range(2 * RMAX + 1):
        beam = beam + taps[:, offset, None, None] * padded[:, :, offset:offset + PCOLS]
    weighted = chan_weight[:, None, None] * beam
    padded = jnp.pad(weighted, ((BW, BW), (0, 0), (0, 0)))
    filtered = weighted
    for offset in range(2 * BW + 1):
        filtered = filtered - band[offset][:, None, None] * padded[offset:offset + NCH]
    comoving = jnp.dot(resample, filtered.reshape(NCH, PROWS * PCOLS), precision=lax.Precision.HIGHEST, preferred_element_type=jnp.float32)
    owners = jnp.arange(N_TILE).astype(jnp.int32)
    onehot = (slab_index[None, :] == owners[:, None]).astype(jnp.int32)
    count = jnp.sum(onehot, axis=1).astype(jnp.int32)
    start = (jnp.cumsum(count) - count).astype(jnp.int32)
    slots = jnp.arange(CAP).astype(jnp.int32)
    source = (start[:, None] + slots[None, :]).astype(jnp.int32)
    valid = slots[None, :] < count[:, None]
    picked = jnp.take(comoving, jnp.clip(source, 0, NOUT - 1).reshape(-1), axis=0)
    picked = jnp.where(valid.reshape(-1)[:, None], picked, jnp.zeros_like(picked))
    return picked.reshape(N_TILE * CAP, PROWS, PCOLS)
```

```python
import functools

import jax
import jax.numpy as jnp
from jax import lax
from jax.experimental import pallas as pl
from jax.experimental.pallas import tpu as pltpu
from jax.sharding import PartitionSpec as P

MESH = pl.DeviceIdType.MESH
RMAX = 4
BW = 8
CAP = 20
LANES = 128
SUB = 8
STEP = 4
TILE_ORDER = (
    (1, 0), (3, 0), (0, 1), (0, 3), (2, 0), (0, 2), (1, 1), (3, 3),
    (1, 3), (3, 1), (2, 2), (1, 2), (3, 2), (2, 1), (2, 3),
)
CHAN_ORDER = ((1, 0), (3, 0), (2, 0), (1, 1), (3, 1), (2, 1), (0, 1))
F32 = jnp.float32
BF16 = jnp.bfloat16


def iota(shape, dim):
    return lax.broadcasted_iota(jnp.int32, shape, dim)


def make_taps(radius_ref, taps_ref, first, chans):
    nch = radius_ref.shape[1]
    pick = iota((chans, nch), 1) == iota((chans, nch), 0) + first
    spread = jnp.sum(jnp.where(pick, radius_ref[...].astype(F32), 0.0), axis=1, keepdims=True)
    sigma = 0.5 * spread + 0.5
    values = []
    for k in range(RMAX + 1):
        value = jnp.exp(-float(k * k) / (2.0 * sigma * sigma))
        values.append(jnp.where(spread >= float(k), value, 0.0))
    total = values[0]
    for k in range(1, RMAX + 1):
        total = total + 2.0 * values[k]
    for k in range(RMAX + 1):
        taps_ref[k] = jnp.broadcast_to(values[k] / total, (chans, LANES))


def make_matrix(weight_ref, band_ref, resample_ref, slab_ref, matrix_ref):
    nch = weight_ref.shape[1]
    nout = resample_ref.shape[0]
    slots = matrix_ref.shape[0]
    distance = iota((nch, nch), 0) - iota((nch, nch), 1)
    filter_t = jnp.where(distance == 0, 1.0, 0.0)
    for o in range(2 * BW + 1):
        filter_t = filter_t - jnp.where(distance == o - BW, band_ref[o : o + 1, :], 0.0)
    combined = lax.dot_general(
        resample_ref[...], filter_t, (((1,), (1,)), ((), ())),
        precision=lax.Precision.HIGHEST, preferred_element_type=F32,
    ) * weight_ref[...]
    high = combined.astype(BF16)
    low = (combined - high.astype(F32)).astype(BF16)
    slab = slab_ref[...].astype(F32)
    eye = iota((nout, nout), 0) == iota((nout, nout), 1)
    slab_col = jnp.sum(jnp.where(eye, slab, 0.0), axis=1, keepdims=True)
    before = jnp.sum(jnp.where(slab_col < slab, 1.0, 0.0), axis=0, keepdims=True)
    rank = iota((1, nout), 1).astype(F32) - before
    code = slab * float(CAP) + rank
    chosen = jnp.where(iota((slots, nout), 0).astype(F32) == code, 1.0, 0.0).astype(BF16)
    matrix_high = jnp.dot(chosen, high, preferred_element_type=F32).astype(BF16)
    matrix_low = jnp.dot(chosen, low, preferred_element_type=F32).astype(BF16)
    matrix_ref[:, 0:nch] = matrix_high
    matrix_ref[:, nch : 2 * nch] = matrix_high
    matrix_ref[:, 2 * nch : 3 * nch] = matrix_low


def kernel(
    sky_ref, mask_ref, radius_ref, weight_ref, band_ref, resample_ref, slab_ref,
    out_ref,
    sky, beam, pencil, outgoing, taps, matrix,
    in_sem, halo_send, halo_recv, chan_send, chan_recv, tile_send, tile_recv,
):
    chan, tile = lax.axis_index("chan"), lax.axis_index("tile")
    n_chan, n_tile = beam.shape[0], outgoing.shape[1] // (CAP * STEP)
    chans, rows = sky_ref.shape[0], sky_ref.shape[1]
    nch = n_chan * chans
    steps = rows // STEP
    block = CAP * STEP

    def chan_peer(offset):
        dy, dc = offset
        return lax.rem(chan // 2 + dy, 4) * 2 + lax.rem(chan + dc, 2)

    def tile_peer(offset):
        dx, dz = offset
        return lax.rem(tile // 4 + dx, 4) * 4 + lax.rem(tile + dz, 4)

    def load(c):
        def one(i, carry):
            row = c * STEP + i
            pltpu.make_async_copy(sky_ref.at[:, row], sky.at[row + RMAX], in_sem.at[c]).start()
            return carry
        lax.fori_loop(0, STEP, one, 0)

    def order(k):
        return lax.rem(k + 1, steps)

    load(0)
    load(steps - 1)
    lax.fori_loop(1, steps - 1, lambda c, carry: (load(c), carry)[1], 0)

    barrier = pltpu.get_barrier_semaphore()
    for offset in CHAN_ORDER:
        pl.semaphore_signal(barrier, inc=1, device_id=(chan_peer(offset), tile), device_id_type=MESH)
    for offset in TILE_ORDER:
        pl.semaphore_signal(barrier, inc=1, device_id=(chan, tile_peer(offset)), device_id_type=MESH)

    make_taps(radius_ref, taps, chan * chans, chans)

    def apply_mask(c):
        piece = sky.at[pl.ds(c * STEP + RMAX, STEP)]
        pltpu.make_async_copy(piece, piece, in_sem.at[c]).wait()

        def one(i, carry):
            row = c * STEP + i
            weight = mask_ref[pl.ds(row, 1), :].astype(F32)
            sky[row + RMAX] = sky[row + RMAX] * weight
            return carry
        lax.fori_loop(0, STEP, one, 0)

    apply_mask(0)
    apply_mask(steps - 1)

    @pl.when(tile == 0)
    def _():
        sky[0:RMAX] = jnp.zeros((RMAX,) + sky.shape[1:], F32)

    @pl.when(tile == n_tile - 1)
    def _():
        sky[rows + RMAX :] = jnp.zeros((RMAX,) + sky.shape[1:], F32)

    pl.semaphore_wait(barrier, len(CHAN_ORDER) + len(TILE_ORDER))

    up = pltpu.make_async_remote_copy(
        sky.at[pl.ds(rows, RMAX)], sky.at[pl.ds(0, RMAX)], halo_send.at[0], halo_recv.at[0],
        device_id=(chan, lax.rem(tile + 1, n_tile)), device_id_type=MESH,
    )
    down = pltpu.make_async_remote_copy(
        sky.at[pl.ds(RMAX, RMAX)], sky.at[pl.ds(rows + RMAX, RMAX)], halo_send.at[1], halo_recv.at[1],
        device_id=(chan, lax.rem(tile + n_tile - 1, n_tile)), device_id_type=MESH,
    )

    @pl.when(tile < n_tile - 1)
    def _():
        up.start()

    @pl.when(tile > 0)
    def _():
        down.start()

    lax.fori_loop(1, steps - 1, lambda c, carry: (apply_mask(c), carry)[1], 0)

    groups = chans // SUB
    lane = iota((SUB, LANES), 1)

    def stencil(c):
        def one(j, carry):
            row = c * STEP + j // groups
            g = pl.multiple_of(lax.rem(j, groups) * SUB, SUB)
            w = [taps[k, pl.ds(g, SUB), :] for k in range(RMAX + 1)]
            along = []
            for q in range(n_chan):
                def at(i):
                    return sky[row + RMAX + i, pl.ds(g, SUB), q * LANES : (q + 1) * LANES]
                value = w[0] * at(0)
                for k in range(1, RMAX + 1):
                    value = value + w[k] * (at(-k) + at(k))
                along.append(value)
            zero = jnp.zeros((SUB, LANES), F32)
            result = [w[0] * a for a in along]
            for k in range(1, RMAX + 1):
                right = [zero] + [pltpu.roll(a, k, 1) for a in along]
                left = [pltpu.roll(a, LANES - k, 1) for a in along] + [zero]
                for q in range(n_chan):
                    r = jnp.where(lane < k, right[q], right[q + 1])
                    s = jnp.where(lane >= LANES - k, left[q + 1], left[q])
                    result[q] = result[q] + w[k] * (r + s)
            for q in range(n_chan):
                beam[q, row, pl.ds(g, SUB), :] = result[q]
            return carry
        lax.fori_loop(0, STEP * groups, one, 0)

    def chan_exchange(c):
        span = pl.ds(c * STEP, STEP)
        place = pl.ds(pl.multiple_of(chan * chans, chans), chans)
        for offset in CHAN_ORDER:
            peer = chan_peer(offset)
            pltpu.make_async_remote_copy(
                beam.at[peer, span], pencil.at[span, place], chan_send, chan_recv.at[c],
                device_id=(peer, tile), device_id_type=MESH,
            ).start()
        pltpu.make_async_copy(beam.at[chan, span], pencil.at[span, place], chan_recv.at[c]).start()

    def multiply(c):
        piece = pencil.at[pl.ds(c * STEP, STEP)]
        pltpu.make_async_copy(piece, piece, chan_recv.at[c]).wait()
        for pair in range(STEP // 2):
            row = c * STEP + 2 * pair
            value = jnp.concatenate([pencil[row], pencil[row + 1]], axis=1)
            high = value.astype(BF16)
            low = (value - high.astype(F32)).astype(BF16)
            spectra = jnp.concatenate([high, low, high], axis=0)
            result = jnp.dot(matrix[...], spectra, preferred_element_type=F32)
            for half in range(2):
                outgoing[c, pl.ds(2 * pair + half, result.shape[0], stride=STEP), :] = result[
                    :, half * LANES : (half + 1) * LANES
                ]

    def tile_exchange(c):
        def source(owner):
            return outgoing.at[c, pl.ds(pl.multiple_of(owner * block, SUB), block)]
        for offset in TILE_ORDER:
            peer = tile_peer(offset)
            pltpu.make_async_remote_copy(
                source(peer), out_ref.at[c, tile], tile_send, tile_recv,
                device_id=(chan, peer), device_id_type=MESH,
            ).start()
        pltpu.make_async_copy(source(tile), out_ref.at[c, tile], tile_recv).start()

    def step(k, carry):
        @pl.when(k == steps - 2)
        def _():
            @pl.when(tile > 0)
            def _():
                up.wait_recv()

            @pl.when(tile < n_tile - 1)
            def _():
                down.wait_recv()

        @pl.when(k < steps)
        def _():
            stencil(order(k))
            chan_exchange(order(k))

        @pl.when(k == 1)
        def _():
            make_matrix(weight_ref, band_ref, resample_ref, slab_ref, matrix)

        @pl.when(k >= 2)
        def _():
            multiply(order(k - 2))
            tile_exchange(order(k - 2))
        return carry

    lax.fori_loop(0, steps + 2, step, 0)

    @pl.when(tile < n_tile - 1)
    def _():
        up.wait_send()

    @pl.when(tile > 0)
    def _():
        down.wait_send()

    sent = beam.at[pl.ds(0, n_chan - 1)]
    pltpu.make_async_copy(sent, sent, chan_send).wait()
    posted = outgoing.at[:, pl.ds(0, (n_tile - 1) * block)]
    pltpu.make_async_copy(posted, posted, tile_send).wait()
    pltpu.make_async_copy(out_ref, out_ref, tile_recv).wait()


def body(n_chan, n_tile, sky_cube, pixel_mask, radius, chan_weight, band, resample, slab_index):
    chans, rows, cols = sky_cube.shape
    steps = rows // STEP
    nch = n_chan * chans
    vmem = pl.BlockSpec(memory_space=pltpu.VMEM)
    hbm = pl.BlockSpec(memory_space=pl.ANY)
    arrived = pl.pallas_call(
        kernel,
        out_shape=jax.ShapeDtypeStruct((steps, n_tile, CAP * STEP, LANES), F32),
        in_specs=[hbm] + [vmem] * 6,
        out_specs=hbm,
        scratch_shapes=[
            pltpu.VMEM((rows + 2 * RMAX, chans, cols), F32),
            pltpu.VMEM((n_chan, rows, chans, LANES), F32),
            pltpu.VMEM((rows, nch, LANES), F32),
            pltpu.VMEM((steps, n_tile * CAP * STEP, LANES), F32),
            pltpu.VMEM((RMAX + 1, chans, LANES), F32),
            pltpu.VMEM((n_tile * CAP, 3 * nch), BF16),
            pltpu.SemaphoreType.DMA((steps,)),
            pltpu.SemaphoreType.DMA((2,)),
            pltpu.SemaphoreType.DMA((2,)),
            pltpu.SemaphoreType.DMA,
            pltpu.SemaphoreType.DMA((steps,)),
            pltpu.SemaphoreType.DMA,
            pltpu.SemaphoreType.DMA,
        ],
        compiler_params=pltpu.CompilerParams(
            collective_id=0, has_side_effects=True, vmem_limit_bytes=40 * 2**20
        ),
        name="slabs",
    )(
        sky_cube, pixel_mask, radius[None, :], chan_weight[None, :], band, resample, slab_index[None, :]
    )
    arrived = arrived.reshape(steps, n_tile, CAP, STEP, LANES)
    return arrived.transpose(2, 1, 0, 3, 4).reshape(CAP, n_tile * rows, LANES)


def solution(mesh):
    in_specs = (P("chan", "tile", None), P("tile", None), P(), P(), P(), P(), P())
    out_specs = P("tile", None, "chan")
    step = functools.partial(body, mesh.shape["chan"], mesh.shape["tile"])
    return jax.shard_map(step, mesh=mesh, in_specs=in_specs, out_specs=out_specs, check_vma=False)
```

```python
import functools

import jax
import jax.numpy as jnp
from jax import lax
from jax.experimental import pallas as pl
from jax.experimental.pallas import tpu as pltpu
from jax.sharding import PartitionSpec as P

MESH = pl.DeviceIdType.MESH
RMAX = 4
BW = 8
CAP = 20
LANES = 128
SUB = 8
STEP = 4
EDGE = RMAX // STEP
LEAD = 2
LIMIT = 50 * 2**20
TILE_ORDER = ((1,2),(2,1),(3,2),(2,3),(2,2),(1,1),(3,3),(1,3),(3,1),(2,0),(0,2),(1,0),(0,1),(3,0),(0,3))
CHAN_ORDER = ((1, 0), (3, 0), (2, 0), (1, 1), (3, 1), (2, 1), (0, 1))
F32 = jnp.float32
BF16 = jnp.bfloat16


def iota(shape, dim):
    return lax.broadcasted_iota(jnp.int32, shape, dim)


def make_taps(radius_ref, taps_ref, first, chans):
    nch = radius_ref.shape[1]
    pick = iota((chans, nch), 1) == iota((chans, nch), 0) + first
    spread = jnp.sum(jnp.where(pick, radius_ref[...].astype(F32), 0.0), axis=1, keepdims=True)
    sigma = 0.5 * spread + 0.5
    values = []
    for k in range(RMAX + 1):
        value = jnp.exp(-float(k * k) / (2.0 * sigma * sigma))
        values.append(jnp.where(spread >= float(k), value, 0.0))
    total = values[0]
    for k in range(1, RMAX + 1):
        total = total + 2.0 * values[k]
    for k in range(RMAX + 1):
        taps_ref[k] = jnp.broadcast_to(values[k] / total, (chans, LANES))


def make_matrix(weight_ref, band_ref, resample_ref, slab_ref, matrix_ref):
    nch = weight_ref.shape[1]
    nout = resample_ref.shape[0]
    slots = matrix_ref.shape[0]
    distance = iota((nch, nch), 0) - iota((nch, nch), 1)
    filter_t = jnp.where(distance == 0, 1.0, 0.0)
    for o in range(2 * BW + 1):
        filter_t = filter_t - jnp.where(distance == o - BW, band_ref[o : o + 1, :], 0.0)
    combined = lax.dot_general(
        resample_ref[...], filter_t, (((1,), (1,)), ((), ())),
        precision=lax.Precision.HIGHEST, preferred_element_type=F32,
    ) * weight_ref[...]
    high = combined.astype(BF16)
    low = (combined - high.astype(F32)).astype(BF16)
    slab = slab_ref[...].astype(F32)
    eye = iota((nout, nout), 0) == iota((nout, nout), 1)
    slab_col = jnp.sum(jnp.where(eye, slab, 0.0), axis=1, keepdims=True)
    before = jnp.sum(jnp.where(slab_col < slab, 1.0, 0.0), axis=0, keepdims=True)
    rank = iota((1, nout), 1).astype(F32) - before
    code = slab * float(CAP) + rank
    chosen = jnp.where(iota((slots, nout), 0).astype(F32) == code, 1.0, 0.0).astype(BF16)
    matrix_high = jnp.dot(chosen, high, preferred_element_type=F32).astype(BF16)
    matrix_low = jnp.dot(chosen, low, preferred_element_type=F32).astype(BF16)
    matrix_ref[:, 0:nch] = matrix_high
    matrix_ref[:, nch : 2 * nch] = matrix_high
    matrix_ref[:, 2 * nch : 3 * nch] = matrix_low


def kernel(
    sky_ref, *rest
):
    small, rest = rest[:6], rest[6:]
    out_ref, rest = rest[0], rest[1:]
    (mask_ref, radius_ref, weight_ref, band_ref, resample_ref, slab_ref), rest = rest[:6], rest[6:]
    (
        sky, beam, pencil, outgoing, taps, matrix,
        small_sem, in_sem, halo_send, halo_recv, chan_send, chan_recv, tile_send, tile_recv,
    ) = rest
    local = (mask_ref, radius_ref, weight_ref, band_ref, resample_ref, slab_ref)
    fetches = [
        pltpu.make_async_copy(source, target, small_sem.at[i])
        for i, (source, target) in enumerate(zip(small, local))
    ]
    chan, tile = lax.axis_index("chan"), lax.axis_index("tile")
    n_chan, n_tile = beam.shape[0], outgoing.shape[1] // (CAP * STEP)
    chans, rows = sky_ref.shape[0], sky_ref.shape[1]
    nch = n_chan * chans
    steps = rows // STEP
    block = CAP * STEP

    def chan_peer(offset):
        dy, dc = offset
        return lax.rem(chan // 2 + dy, 4) * 2 + lax.rem(chan + dc, 2)

    def tile_peer(offset):
        dx, dz = offset
        return lax.rem(tile // 4 + dx, 4) * 4 + lax.rem(tile + dz, 4)

    def load(c):
        def one(i, carry):
            row = c * STEP + i
            pltpu.make_async_copy(sky_ref.at[:, row], sky.at[row + RMAX], in_sem.at[c]).start()
            return carry
        lax.fori_loop(0, STEP, one, 0)

    def order(k):
        return lax.rem(k + EDGE, steps)

    barrier = pltpu.get_barrier_semaphore()
    for offset in TILE_ORDER:
        pl.semaphore_signal(barrier, inc=1, device_id=(chan, tile_peer(offset)), device_id_type=MESH)
    for offset in CHAN_ORDER:
        pl.semaphore_signal(barrier, inc=1, device_id=(chan_peer(offset), tile), device_id_type=MESH)

    fetches[0].start()
    for c in range(EDGE):
        load(c)
        load(steps - 1 - c)
    for c in range(EDGE, 3 * EDGE):
        load(c)
    for fetch in fetches[1:]:
        fetch.start()

    def apply_mask(c):
        piece = sky.at[pl.ds(c * STEP + RMAX, STEP)]
        pltpu.make_async_copy(piece, piece, in_sem.at[c]).wait()

        def one(i, carry):
            row = c * STEP + i
            weight = mask_ref[pl.ds(row, 1), :].astype(F32)
            sky[row + RMAX] = sky[row + RMAX] * weight
            return carry
        lax.fori_loop(0, STEP, one, 0)

    @pl.when(tile == 0)
    def _():
        sky[0:RMAX] = jnp.zeros((RMAX,) + sky.shape[1:], F32)

    @pl.when(tile == n_tile - 1)
    def _():
        sky[rows + RMAX :] = jnp.zeros((RMAX,) + sky.shape[1:], F32)

    fetches[0].wait()
    for c in range(EDGE):
        apply_mask(c)
        apply_mask(steps - 1 - c)
    pl.semaphore_wait(barrier, len(CHAN_ORDER) + len(TILE_ORDER))

    up = pltpu.make_async_remote_copy(
        sky.at[pl.ds(rows, RMAX)], sky.at[pl.ds(0, RMAX)], halo_send.at[0], halo_recv.at[0],
        device_id=(chan, lax.rem(tile + 1, n_tile)), device_id_type=MESH,
    )
    down = pltpu.make_async_remote_copy(
        sky.at[pl.ds(RMAX, RMAX)], sky.at[pl.ds(rows + RMAX, RMAX)], halo_send.at[1], halo_recv.at[1],
        device_id=(chan, lax.rem(tile + n_tile - 1, n_tile)), device_id_type=MESH,
    )

    @pl.when(tile < n_tile - 1)
    def _():
        up.start()

    @pl.when(tile > 0)
    def _():
        down.start()

    lax.fori_loop(3 * EDGE, steps - EDGE, lambda c, carry: (load(c), carry)[1], 0)
    for fetch in fetches[1:]:
        fetch.wait()
    make_taps(radius_ref, taps, chan * chans, chans)
    for c in range(EDGE, 2 * EDGE):
        apply_mask(c)

    groups = chans // SUB
    lane = iota((SUB, LANES), 1)

    def columns(w, along, g, row):
        zero = jnp.zeros((SUB, LANES), F32)
        last = len(along)
        ahead = [pltpu.roll(a, 1, 1) for a in along] + [zero]
        behind = [pltpu.roll(a, LANES - 1, 1) for a in along] + [zero]
        before = [jnp.where(lane < 1, ahead[q - 1], ahead[q]) for q in range(last + 1)]
        after = [jnp.where(lane >= LANES - 1, behind[(q + 1) % (last + 1)], behind[q]) for q in range(last + 1)]
        middle = [w[3] * a for a in along]
        upper = [w[2] * before[q] + (middle[q] + w[4] * after[q]) for q in range(last)] + [w[2] * before[last]]
        lower = [w[4] * before[q] + (middle[q] + w[2] * after[q]) for q in range(last)] + [w[2] * after[last]]
        upper = [pltpu.roll(a, LANES - 3, 1) for a in upper]
        lower = [pltpu.roll(a, 3, 1) for a in lower]
        for q in range(last):
            u = jnp.where(lane >= LANES - 3, upper[q + 1], upper[q])
            v = jnp.where(lane < 3, lower[q - 1], lower[q])
            beam[q, row, pl.ds(g, SUB), :] = (w[0] * along[q] + w[1] * (before[q] + after[q])) + (u + v)

    def rows_pass(w, row, g):
        along = []
        for q in range(n_chan):
            def at(i):
                return sky[row + RMAX + i, pl.ds(g, SUB), q * LANES : (q + 1) * LANES]
            value = w[0] * at(0)
            for k in range(1, RMAX + 1):
                value = value + w[k] * (at(-k) + at(k))
            along.append(value)
        return along

    def stencil(c):
        def one(j, carry):
            for u in range(4):
                jj = j * 4 + u
                row = c * STEP + jj // groups
                g = pl.multiple_of(lax.rem(jj, groups) * SUB, SUB)
                w = [taps[k, pl.ds(g, SUB), :] for k in range(RMAX + 1)]
                columns(w, rows_pass(w, row, g), g, row)
            return carry
        lax.fori_loop(0, STEP * groups // 4, one, 0)

    def chan_exchange(c):
        span = pl.ds(c * STEP, STEP)
        place = pl.ds(pl.multiple_of(chan * chans, chans), chans)
        for offset in CHAN_ORDER:
            peer = chan_peer(offset)
            pltpu.make_async_remote_copy(
                beam.at[peer, span], pencil.at[span, place], chan_send, chan_recv.at[c],
                device_id=(peer, tile), device_id_type=MESH,
            ).start()
        pltpu.make_async_copy(beam.at[chan, span], pencil.at[span, place], chan_recv.at[c]).start()

    def multiply(c):
        piece = pencil.at[pl.ds(c * STEP, STEP)]
        pltpu.make_async_copy(piece, piece, chan_recv.at[c]).wait()
        for pair in range(STEP // 2):
            row = c * STEP + 2 * pair
            value = jnp.concatenate([pencil[row], pencil[row + 1]], axis=1)
            high = value.astype(BF16)
            low = (value - high.astype(F32)).astype(BF16)
            spectra = jnp.concatenate([high, low, high], axis=0)
            result = jnp.dot(matrix[...], spectra, preferred_element_type=F32)
            for half in range(2):
                outgoing[c, pl.ds(2 * pair + half, result.shape[0], stride=STEP), :] = result[
                    :, half * LANES : (half + 1) * LANES
                ]

    def tile_exchange(c):
        def source(owner):
            return outgoing.at[c, pl.ds(pl.multiple_of(owner * block, SUB), block)].reshape(CAP, STEP, LANES)
        for offset in TILE_ORDER:
            peer = tile_peer(offset)
            pltpu.make_async_remote_copy(
                source(peer), out_ref.at[:, tile, c], tile_send, tile_recv,
                device_id=(chan, peer), device_id_type=MESH,
            ).start()
        pltpu.make_async_copy(source(tile), out_ref.at[:, tile, c], tile_recv).start()

    def step(k, carry):
        @pl.when(k == steps - 2 * EDGE)
        def _():
            @pl.when(tile > 0)
            def _():
                up.wait_recv()

            @pl.when(tile < n_tile - 1)
            def _():
                down.wait_recv()

        @pl.when(k < steps)
        def _():
            @pl.when(k < steps - 3 * EDGE)
            def _():
                apply_mask(order(k) + EDGE)

            stencil(order(k))
            chan_exchange(order(k))

        @pl.when(k == 1)
        def _():
            make_matrix(weight_ref, band_ref, resample_ref, slab_ref, matrix)

        @pl.when(k >= LEAD)
        def _():
            multiply(order(k - LEAD))
            tile_exchange(order(k - LEAD))
        return carry

    lax.fori_loop(0, steps + LEAD, step, 0)

    @pl.when(tile < n_tile - 1)
    def _():
        up.wait_send()

    @pl.when(tile > 0)
    def _():
        down.wait_send()

    sent = beam.at[pl.ds(0, n_chan - 1)]
    pltpu.make_async_copy(sent, sent, chan_send).wait()
    posted = outgoing.at[:, pl.ds(0, (n_tile - 1) * block)]
    pltpu.make_async_copy(posted, posted, tile_send).wait()
    pltpu.make_async_copy(out_ref, out_ref, tile_recv).wait()


def store(arrived_ref, out_ref, sem):
    copies = [pltpu.make_async_copy(arrived_ref.at[s], out_ref.at[s], sem.at[s]) for s in range(CAP)]
    for copy in copies:
        copy.start()
    for copy in copies:
        copy.wait()


def body(n_chan, n_tile, sky_cube, pixel_mask, radius, chan_weight, band, resample, slab_index):
    chans, rows, cols = sky_cube.shape
    steps = rows // STEP
    nch = n_chan * chans
    hbm = pl.BlockSpec(memory_space=pltpu.HBM)
    arrived = pl.pallas_call(
        kernel,
        out_shape=pltpu.VMEM((CAP, n_tile, steps, STEP, LANES), F32),
        in_specs=[hbm] * 7,
        out_specs=pl.BlockSpec(memory_space=pl.ANY),
        scratch_shapes=[
            pltpu.VMEM((rows, cols), jnp.int32),
            pltpu.VMEM((1, nch), jnp.int32),
            pltpu.VMEM((1, nch), F32),
            pltpu.VMEM(band.shape, F32),
            pltpu.VMEM(resample.shape, F32),
            pltpu.VMEM((1, slab_index.shape[0]), jnp.int32),
            pltpu.VMEM((rows + 2 * RMAX, chans, cols), F32),
            pltpu.VMEM((n_chan, rows, chans, LANES), F32),
            pltpu.VMEM((rows, nch, LANES), F32),
            pltpu.VMEM((steps, n_tile * CAP * STEP, LANES), F32),
            pltpu.VMEM((RMAX + 1, chans, LANES), F32),
            pltpu.VMEM((n_tile * CAP, 3 * nch), BF16),
            pltpu.SemaphoreType.DMA((6,)),
            pltpu.SemaphoreType.DMA((steps,)),
            pltpu.SemaphoreType.DMA((2,)),
            pltpu.SemaphoreType.DMA((2,)),
            pltpu.SemaphoreType.DMA,
            pltpu.SemaphoreType.DMA((steps,)),
            pltpu.SemaphoreType.DMA,
            pltpu.SemaphoreType.DMA,
        ],
        compiler_params=pltpu.CompilerParams(
            collective_id=0, has_side_effects=True, vmem_limit_bytes=LIMIT
        ),
        name="slabs",
    )(
        *[
            pltpu.with_memory_space_constraint(x, pltpu.HBM)
            for x in (
                sky_cube, pixel_mask, radius[None, :], chan_weight[None, :], band, resample, slab_index[None, :]
            )
        ]
    )
    placed = pl.pallas_call(
        store,
        out_shape=jax.ShapeDtypeStruct(arrived.shape, F32),
        in_specs=[pl.BlockSpec(memory_space=pltpu.VMEM)],
        out_specs=hbm,
        scratch_shapes=[pltpu.SemaphoreType.DMA((CAP,))],
        compiler_params=pltpu.CompilerParams(vmem_limit_bytes=2**20),
        name="store",
    )(pltpu.with_memory_space_constraint(arrived, pltpu.VMEM))
    return placed.reshape(CAP, n_tile * rows, LANES)


def solution(mesh):
    in_specs = (P("chan", "tile", None), P("tile", None), P(), P(), P(), P(), P())
    out_specs = P("tile", None, "chan")
    step = functools.partial(body, mesh.shape["chan"], mesh.shape["tile"])
    return jax.shard_map(step, mesh=mesh, in_specs=in_specs, out_specs=out_specs, check_vma=False)
```

```python
import functools

import jax
import jax.numpy as jnp
from jax import lax
from jax.experimental import pallas as pl
from jax.experimental.pallas import tpu as pltpu
from jax.sharding import PartitionSpec as P

MESH = pl.DeviceIdType.MESH
RMAX = 4
BW = 8
CAP = 20
LANES = 128
SUB = 8
STEP = 4
EDGE = RMAX // STEP
LEAD = 2
LIMIT = 50 * 2**20
TILE_ORDER = ((1,2),(2,1),(3,2),(2,3),(2,2),(1,1),(3,3),(1,3),(3,1),(2,0),(0,2),(1,0),(0,1),(3,0),(0,3))
CHAN_ORDER = ((1, 0), (3, 0), (2, 0), (1, 1), (3, 1), (2, 1), (0, 1))
F32 = jnp.float32
BF16 = jnp.bfloat16
PRODUCTS = ((0, 0), (0, 1), (1, 0), (1, 1), (0, 2), (2, 0))


def iota(shape, dim):
    return lax.broadcasted_iota(jnp.int32, shape, dim)


def split(value):
    parts = []
    for _ in range(3):
        part = value.astype(BF16)
        value = value - part.astype(F32)
        parts.append(part)
    return parts


def make_taps(radius_ref, taps_ref, first, chans):
    nch = radius_ref.shape[1]
    pick = iota((chans, nch), 1) == iota((chans, nch), 0) + first
    spread = jnp.sum(jnp.where(pick, radius_ref[...].astype(F32), 0.0), axis=1, keepdims=True)
    sigma = 0.5 * spread + 0.5
    values = []
    for k in range(RMAX + 1):
        value = jnp.exp(-float(k * k) / (2.0 * sigma * sigma))
        values.append(jnp.where(spread >= float(k), value, 0.0))
    total = values[0]
    for k in range(1, RMAX + 1):
        total = total + 2.0 * values[k]
    for k in range(RMAX + 1):
        taps_ref[k] = jnp.broadcast_to(values[k] / total, (chans, LANES))


def make_matrix(weight_ref, band_ref, resample_ref, slab_ref, matrix_ref):
    nch = weight_ref.shape[1]
    nout = resample_ref.shape[0]
    slots = matrix_ref.shape[0]
    distance = iota((nch, nch), 0) - iota((nch, nch), 1)
    filter_t = jnp.where(distance == 0, 1.0, 0.0)
    for o in range(2 * BW + 1):
        filter_t = filter_t - jnp.where(distance == o - BW, band_ref[o : o + 1, :], 0.0)
    combined = lax.dot_general(
        resample_ref[...], filter_t, (((1,), (1,)), ((), ())),
        precision=lax.Precision.HIGHEST, preferred_element_type=F32,
    ) * weight_ref[...]
    parts = split(combined)
    slab = slab_ref[...].astype(F32)
    eye = iota((nout, nout), 0) == iota((nout, nout), 1)
    slab_col = jnp.sum(jnp.where(eye, slab, 0.0), axis=1, keepdims=True)
    before = jnp.sum(jnp.where(slab_col < slab, 1.0, 0.0), axis=0, keepdims=True)
    rank = iota((1, nout), 1).astype(F32) - before
    code = slab * float(CAP) + rank
    chosen = jnp.where(iota((slots, nout), 0).astype(F32) == code, 1.0, 0.0).astype(BF16)
    picked = [jnp.dot(chosen, part, preferred_element_type=F32).astype(BF16) for part in parts]
    for i, (left, _) in enumerate(PRODUCTS):
        matrix_ref[:, i * nch : (i + 1) * nch] = picked[left]


def kernel(
    sky_ref, *rest
):
    small, rest = rest[:6], rest[6:]
    out_ref, rest = rest[0], rest[1:]
    (mask_ref, radius_ref, weight_ref, band_ref, resample_ref, slab_ref), rest = rest[:6], rest[6:]
    (
        sky, beam, pencil, outgoing, taps, matrix,
        small_sem, in_sem, halo_send, halo_recv, chan_send, chan_recv, tile_send, tile_recv,
    ) = rest
    local = (mask_ref, radius_ref, weight_ref, band_ref, resample_ref, slab_ref)
    fetches = [
        pltpu.make_async_copy(source, target, small_sem.at[i])
        for i, (source, target) in enumerate(zip(small, local))
    ]
    chan, tile = lax.axis_index("chan"), lax.axis_index("tile")
    n_chan, n_tile = beam.shape[0], out_ref.shape[1]
    chans, rows = sky_ref.shape[0], sky_ref.shape[1]
    nch = n_chan * chans
    steps = rows // STEP
    block = CAP * STEP

    def chan_peer(offset):
        dy, dc = offset
        return lax.rem(chan // 2 + dy, 4) * 2 + lax.rem(chan + dc, 2)

    def tile_peer(offset):
        dx, dz = offset
        return lax.rem(tile // 4 + dx, 4) * 4 + lax.rem(tile + dz, 4)

    def load(c):
        def one(i, carry):
            row = c * STEP + i
            pltpu.make_async_copy(sky_ref.at[:, row], sky.at[row + RMAX], in_sem.at[c]).start()
            return carry
        lax.fori_loop(0, STEP, one, 0)

    def order(k):
        return lax.rem(k + EDGE, steps)

    barrier = pltpu.get_barrier_semaphore()
    for offset in TILE_ORDER:
        pl.semaphore_signal(barrier, inc=1, device_id=(chan, tile_peer(offset)), device_id_type=MESH)
    for offset in CHAN_ORDER:
        pl.semaphore_signal(barrier, inc=1, device_id=(chan_peer(offset), tile), device_id_type=MESH)

    fetches[0].start()
    for c in range(EDGE):
        load(c)
        load(steps - 1 - c)
    for c in range(EDGE, 3 * EDGE):
        load(c)
    for fetch in fetches[1:]:
        fetch.start()

    def apply_mask(c):
        piece = sky.at[pl.ds(c * STEP + RMAX, STEP)]
        pltpu.make_async_copy(piece, piece, in_sem.at[c]).wait()

        def one(i, carry):
            row = c * STEP + i
            weight = mask_ref[pl.ds(row, 1), :].astype(F32)
            sky[row + RMAX] = sky[row + RMAX] * weight
            return carry
        lax.fori_loop(0, STEP, one, 0)

    @pl.when(tile == 0)
    def _():
        sky[0:RMAX] = jnp.zeros((RMAX,) + sky.shape[1:], F32)

    @pl.when(tile == n_tile - 1)
    def _():
        sky[rows + RMAX :] = jnp.zeros((RMAX,) + sky.shape[1:], F32)

    fetches[0].wait()
    for c in range(EDGE):
        apply_mask(c)
        apply_mask(steps - 1 - c)
    pl.semaphore_wait(barrier, len(CHAN_ORDER) + len(TILE_ORDER))

    up = pltpu.make_async_remote_copy(
        sky.at[pl.ds(rows, RMAX)], sky.at[pl.ds(0, RMAX)], halo_send.at[0], halo_recv.at[0],
        device_id=(chan, lax.rem(tile + 1, n_tile)), device_id_type=MESH,
    )
    down = pltpu.make_async_remote_copy(
        sky.at[pl.ds(RMAX, RMAX)], sky.at[pl.ds(rows + RMAX, RMAX)], halo_send.at[1], halo_recv.at[1],
        device_id=(chan, lax.rem(tile + n_tile - 1, n_tile)), device_id_type=MESH,
    )

    @pl.when(tile < n_tile - 1)
    def _():
        up.start()

    @pl.when(tile > 0)
    def _():
        down.start()

    for fetch in fetches[1:]:
        fetch.wait()
    make_taps(radius_ref, taps, chan * chans, chans)
    for c in range(EDGE, 2 * EDGE):
        apply_mask(c)

    groups = chans // SUB
    lane = iota((SUB, LANES), 1)

    def columns(w, along, g, row):
        zero = jnp.zeros((SUB, LANES), F32)
        last = len(along)
        ahead = [pltpu.roll(a, 1, 1) for a in along] + [zero]
        behind = [pltpu.roll(a, LANES - 1, 1) for a in along] + [zero]
        before = [jnp.where(lane < 1, ahead[q - 1], ahead[q]) for q in range(last + 1)]
        after = [jnp.where(lane >= LANES - 1, behind[(q + 1) % (last + 1)], behind[q]) for q in range(last + 1)]
        middle = [w[3] * a for a in along]
        upper = [w[2] * before[q] + (middle[q] + w[4] * after[q]) for q in range(last)] + [w[2] * before[last]]
        lower = [w[4] * before[q] + (middle[q] + w[2] * after[q]) for q in range(last)] + [w[2] * after[last]]
        upper = [pltpu.roll(a, LANES - 3, 1) for a in upper]
        lower = [pltpu.roll(a, 3, 1) for a in lower]
        for q in range(last):
            u = jnp.where(lane >= LANES - 3, upper[q + 1], upper[q])
            v = jnp.where(lane < 3, lower[q - 1], lower[q])
            beam[q, row, pl.ds(g, SUB), :] = (w[0] * along[q] + w[1] * (before[q] + after[q])) + (u + v)

    def rows_pass(w, row, g):
        along = []
        for q in range(n_chan):
            def at(i):
                return sky[row + RMAX + i, pl.ds(g, SUB), q * LANES : (q + 1) * LANES]
            value = w[0] * at(0)
            for k in range(1, RMAX + 1):
                value = value + w[k] * (at(-k) + at(k))
            along.append(value)
        return along

    def stencil(c):
        def one(j, carry):
            for u in range(8):
                jj = j * 8 + u
                row = c * STEP + jj // groups
                g = pl.multiple_of(lax.rem(jj, groups) * SUB, SUB)
                w = [taps[k, pl.ds(g, SUB), :] for k in range(RMAX + 1)]
                columns(w, rows_pass(w, row, g), g, row)
            return carry
        lax.fori_loop(0, STEP * groups // 8, one, 0)

    def chan_exchange(c):
        span = pl.ds(c * STEP, STEP)
        place = pl.ds(pl.multiple_of(chan * chans, chans), chans)
        for offset in CHAN_ORDER:
            peer = chan_peer(offset)
            pltpu.make_async_remote_copy(
                beam.at[peer, span], pencil.at[span, place], chan_send, chan_recv.at[c],
                device_id=(peer, tile), device_id_type=MESH,
            ).start()
        pltpu.make_async_copy(beam.at[chan, span], pencil.at[span, place], chan_recv.at[c]).start()

    def multiply(c):
        piece = pencil.at[pl.ds(c * STEP, STEP)]
        pltpu.make_async_copy(piece, piece, chan_recv.at[c]).wait()
        for pair in range(STEP // 2):
            row = c * STEP + 2 * pair
            value = jnp.concatenate([pencil[row], pencil[row + 1]], axis=1)
            parts = split(value)
            spectra = jnp.concatenate([parts[right] for _, right in PRODUCTS], axis=0)
            result = jnp.dot(matrix[...], spectra, preferred_element_type=F32)
            for half in range(2):
                outgoing[c, pl.ds(2 * pair + half, result.shape[0], stride=STEP), :] = result[
                    :, half * LANES : (half + 1) * LANES
                ]

    def tile_exchange(c):
        def source(owner):
            return outgoing.at[c, pl.ds(pl.multiple_of(owner * block, SUB), block)].reshape(CAP, STEP, LANES)
        for offset in TILE_ORDER:
            peer = tile_peer(offset)
            pltpu.make_async_remote_copy(
                source(peer), out_ref.at[:, tile, c], tile_send, tile_recv,
                device_id=(chan, peer), device_id_type=MESH,
            ).start()
        pltpu.make_async_copy(source(tile), out_ref.at[:, tile, c], tile_recv).start()

    def step(k, carry):
        @pl.when(k == steps - 2 * EDGE)
        def _():
            @pl.when(tile > 0)
            def _():
                up.wait_recv()

            @pl.when(tile < n_tile - 1)
            def _():
                down.wait_recv()

        @pl.when(k < steps)
        def _():
            @pl.when(k < steps - 3 * EDGE)
            def _():
                apply_mask(order(k) + EDGE)

            stencil(order(k))
            chan_exchange(order(k))

        @pl.when(k == 0)
        def _():
            lax.fori_loop(3 * EDGE, steps - EDGE, lambda c, carry: (load(c), carry)[1], 0)

        @pl.when(k == 1)
        def _():
            make_matrix(weight_ref, band_ref, resample_ref, slab_ref, matrix)

        @pl.when(k >= LEAD)
        def _():
            multiply(order(k - LEAD))
            tile_exchange(order(k - LEAD))
        return carry

    lax.fori_loop(0, steps + LEAD, step, 0)

    @pl.when(tile < n_tile - 1)
    def _():
        up.wait_send()

    @pl.when(tile > 0)
    def _():
        down.wait_send()

    sent = beam.at[pl.ds(0, n_chan - 1)]
    pltpu.make_async_copy(sent, sent, chan_send).wait()
    posted = outgoing.at[:, pl.ds(0, (n_tile - 1) * block)]
    pltpu.make_async_copy(posted, posted, tile_send).wait()
    pltpu.make_async_copy(out_ref, out_ref, tile_recv).wait()


def body(n_chan, n_tile, sky_cube, pixel_mask, radius, chan_weight, band, resample, slab_index):
    chans, rows, cols = sky_cube.shape
    steps = rows // STEP
    nch = n_chan * chans
    hbm = pl.BlockSpec(memory_space=pltpu.HBM)
    arrived = pl.pallas_call(
        kernel,
        out_shape=pltpu.VMEM((CAP, n_tile, steps, STEP, LANES), F32),
        in_specs=[hbm] * 7,
        out_specs=pl.BlockSpec(memory_space=pl.ANY),
        scratch_shapes=[
            pltpu.VMEM((rows, cols), jnp.int32),
            pltpu.VMEM((1, nch), jnp.int32),
            pltpu.VMEM((1, nch), F32),
            pltpu.VMEM(band.shape, F32),
            pltpu.VMEM(resample.shape, F32),
            pltpu.VMEM((1, slab_index.shape[0]), jnp.int32),
            pltpu.VMEM((rows + 2 * RMAX, chans, cols), F32),
            pltpu.VMEM((n_chan, rows, chans, LANES), F32),
            pltpu.VMEM((rows, nch, LANES), F32),
            pltpu.VMEM((steps, n_tile * CAP * STEP + SUB, LANES), F32),
            pltpu.VMEM((RMAX + 1, chans, LANES), F32),
            pltpu.VMEM((n_tile * CAP, len(PRODUCTS) * nch), BF16),
            pltpu.SemaphoreType.DMA((6,)),
            pltpu.SemaphoreType.DMA((steps,)),
            pltpu.SemaphoreType.DMA((2,)),
            pltpu.SemaphoreType.DMA((2,)),
            pltpu.SemaphoreType.DMA,
            pltpu.SemaphoreType.DMA((steps,)),
            pltpu.SemaphoreType.DMA,
            pltpu.SemaphoreType.DMA,
        ],
        compiler_params=pltpu.CompilerParams(
            collective_id=0, has_side_effects=True, vmem_limit_bytes=LIMIT
        ),
        name="slabs",
    )(
        *[
            pltpu.with_memory_space_constraint(x, pltpu.HBM)
            for x in (
                sky_cube, pixel_mask, radius[None, :], chan_weight[None, :], band, resample, slab_index[None, :]
            )
        ]
    )
    return arrived.reshape(CAP, n_tile * rows, LANES)


def solution(mesh):
    in_specs = (P("chan", "tile", None), P("tile", None), P(), P(), P(), P(), P())
    out_specs = P("tile", None, "chan")
    step = functools.partial(body, mesh.shape["chan"], mesh.shape["tile"])
    return jax.shard_map(step, mesh=mesh, in_specs=in_specs, out_specs=out_specs, check_vma=False)
```

```python
import functools

import jax
import jax.numpy as jnp
from jax import lax
from jax.experimental import pallas as pl
from jax.experimental.pallas import tpu as pltpu
from jax.sharding import PartitionSpec as P

MESH = pl.DeviceIdType.MESH
RMAX = 4
BW = 8
CAP = 20
LANES = 128
SUB = 8
STEP = 4
EDGE = RMAX // STEP
LEAD = 2
LIMIT = 50 * 2**20
TILE_ORDER = ((1,2),(2,1),(3,2),(2,3),(2,2),(1,1),(3,3),(1,3),(3,1),(2,0),(0,2),(1,0),(0,1),(3,0),(0,3))
CHAN_ORDER = ((1, 0), (3, 0), (2, 0), (1, 1), (3, 1), (2, 1), (0, 1))
F32 = jnp.float32
BF16 = jnp.bfloat16
PRODUCTS = ((0, 0), (0, 1), (1, 0), (1, 1), (0, 2), (2, 0))


def iota(shape, dim):
    return lax.broadcasted_iota(jnp.int32, shape, dim)


def split(value):
    parts = []
    for _ in range(3):
        part = value.astype(BF16)
        value = value - part.astype(F32)
        parts.append(part)
    return parts


def make_taps(radius_ref, taps_ref, first, chans):
    nch = radius_ref.shape[1]
    pick = iota((chans, nch), 1) == iota((chans, nch), 0) + first
    spread = jnp.sum(jnp.where(pick, radius_ref[...].astype(F32), 0.0), axis=1, keepdims=True)
    sigma = 0.5 * spread + 0.5
    values = []
    for k in range(RMAX + 1):
        value = jnp.exp(-float(k * k) / (2.0 * sigma * sigma))
        values.append(jnp.where(spread >= float(k), value, 0.0))
    total = values[0]
    for k in range(1, RMAX + 1):
        total = total + 2.0 * values[k]
    for k in range(RMAX + 1):
        taps_ref[k] = jnp.broadcast_to(values[k] / total, (chans, LANES))


def make_matrix(weight_ref, band_ref, resample_ref, slab_ref, matrix_ref):
    nch = weight_ref.shape[1]
    nout = resample_ref.shape[0]
    slots = matrix_ref.shape[0]
    distance = iota((nch, nch), 0) - iota((nch, nch), 1)
    filter_t = jnp.where(distance == 0, 1.0, 0.0)
    for o in range(2 * BW + 1):
        filter_t = filter_t - jnp.where(distance == o - BW, band_ref[o : o + 1, :], 0.0)
    combined = lax.dot_general(
        resample_ref[...], filter_t, (((1,), (1,)), ((), ())),
        precision=lax.Precision.HIGHEST, preferred_element_type=F32,
    ) * weight_ref[...]
    parts = split(combined)
    slab = slab_ref[...].astype(F32)
    eye = iota((nout, nout), 0) == iota((nout, nout), 1)
    slab_col = jnp.sum(jnp.where(eye, slab, 0.0), axis=1, keepdims=True)
    before = jnp.sum(jnp.where(slab_col < slab, 1.0, 0.0), axis=0, keepdims=True)
    rank = iota((1, nout), 1).astype(F32) - before
    code = slab * float(CAP) + rank
    chosen = jnp.where(iota((slots, nout), 0).astype(F32) == code, 1.0, 0.0).astype(BF16)
    picked = [jnp.dot(chosen, part, preferred_element_type=F32).astype(BF16) for part in parts]
    for i, (left, _) in enumerate(PRODUCTS):
        matrix_ref[:, i * nch : (i + 1) * nch] = picked[left]


def kernel(
    sky_ref, *rest
):
    small, rest = rest[:6], rest[6:]
    out_ref, rest = rest[0], rest[1:]
    (mask_ref, radius_ref, weight_ref, band_ref, resample_ref, slab_ref), rest = rest[:6], rest[6:]
    (
        sky, beam, pencil, outgoing, taps, matrix,
        small_sem, in_sem, halo_send, halo_recv, chan_send, chan_recv, tile_send, tile_recv,
    ) = rest
    local = (mask_ref, radius_ref, weight_ref, band_ref, resample_ref, slab_ref)
    fetches = [
        pltpu.make_async_copy(source, target, small_sem.at[i])
        for i, (source, target) in enumerate(zip(small, local))
    ]
    chan, tile = lax.axis_index("chan"), lax.axis_index("tile")
    n_chan, n_tile = beam.shape[0], out_ref.shape[1]
    chans, rows = sky_ref.shape[0], sky_ref.shape[1]
    nch = n_chan * chans
    steps = rows // STEP
    block = CAP * STEP

    def chan_peer(offset):
        dy, dc = offset
        return lax.rem(chan // 2 + dy, 4) * 2 + lax.rem(chan + dc, 2)

    def tile_peer(offset):
        dx, dz = offset
        return lax.rem(tile // 4 + dx, 4) * 4 + lax.rem(tile + dz, 4)

    def load(c):
        def one(i, carry):
            row = c * STEP + i
            pltpu.make_async_copy(sky_ref.at[:, row], sky.at[row + RMAX], in_sem.at[c]).start()
            return carry
        lax.fori_loop(0, STEP, one, 0)

    def order(k):
        return lax.rem(k + EDGE, steps)

    fetches[0].start()
    for c in range(EDGE):
        load(c)
        load(steps - 1 - c)
    barrier = pltpu.get_barrier_semaphore()
    for offset in TILE_ORDER:
        pl.semaphore_signal(barrier, inc=1, device_id=(chan, tile_peer(offset)), device_id_type=MESH)
    for offset in CHAN_ORDER:
        pl.semaphore_signal(barrier, inc=1, device_id=(chan_peer(offset), tile), device_id_type=MESH)

    for c in range(EDGE, 3 * EDGE):
        load(c)
    for fetch in fetches[1:]:
        fetch.start()

    def apply_mask(c):
        piece = sky.at[pl.ds(c * STEP + RMAX, STEP)]
        pltpu.make_async_copy(piece, piece, in_sem.at[c]).wait()

        def one(i, carry):
            row = c * STEP + i
            weight = mask_ref[pl.ds(row, 1), :].astype(F32)
            sky[row + RMAX] = sky[row + RMAX] * weight
            return carry
        lax.fori_loop(0, STEP, one, 0)

    @pl.when(tile == 0)
    def _():
        sky[0:RMAX] = jnp.zeros((RMAX,) + sky.shape[1:], F32)

    @pl.when(tile == n_tile - 1)
    def _():
        sky[rows + RMAX :] = jnp.zeros((RMAX,) + sky.shape[1:], F32)

    fetches[0].wait()
    for c in range(EDGE):
        apply_mask(c)
        apply_mask(steps - 1 - c)
    pl.semaphore_wait(barrier, len(CHAN_ORDER) + len(TILE_ORDER))

    up = pltpu.make_async_remote_copy(
        sky.at[pl.ds(rows, RMAX)], sky.at[pl.ds(0, RMAX)], halo_send.at[0], halo_recv.at[0],
        device_id=(chan, lax.rem(tile + 1, n_tile)), device_id_type=MESH,
    )
    down = pltpu.make_async_remote_copy(
        sky.at[pl.ds(RMAX, RMAX)], sky.at[pl.ds(rows + RMAX, RMAX)], halo_send.at[1], halo_recv.at[1],
        device_id=(chan, lax.rem(tile + n_tile - 1, n_tile)), device_id_type=MESH,
    )

    @pl.when(tile < n_tile - 1)
    def _():
        up.start()

    @pl.when(tile > 0)
    def _():
        down.start()

    for fetch in fetches[1:]:
        fetch.wait()
    make_taps(radius_ref, taps, chan * chans, chans)
    for c in range(EDGE, 2 * EDGE):
        apply_mask(c)

    groups = chans // SUB
    lane = iota((SUB, LANES), 1)

    def columns(w, along, g, row):
        zero = jnp.zeros((SUB, LANES), F32)
        last = len(along)
        ahead = [pltpu.roll(a, 1, 1) for a in along] + [zero]
        behind = [pltpu.roll(a, LANES - 1, 1) for a in along] + [zero]
        before = [jnp.where(lane < 1, ahead[q - 1], ahead[q]) for q in range(last + 1)]
        after = [jnp.where(lane >= LANES - 1, behind[(q + 1) % (last + 1)], behind[q]) for q in range(last + 1)]
        middle = [w[3] * a for a in along]
        upper = [w[2] * before[q] + (middle[q] + w[4] * after[q]) for q in range(last)] + [w[2] * before[last]]
        lower = [w[4] * before[q] + (middle[q] + w[2] * after[q]) for q in range(last)] + [w[2] * after[last]]
        upper = [pltpu.roll(a, LANES - 3, 1) for a in upper]
        lower = [pltpu.roll(a, 3, 1) for a in lower]
        for q in range(last):
            u = jnp.where(lane >= LANES - 3, upper[q + 1], upper[q])
            v = jnp.where(lane < 3, lower[q - 1], lower[q])
            beam[q, row, pl.ds(g, SUB), :] = (w[0] * along[q] + w[1] * (before[q] + after[q])) + (u + v)

    def rows_pass(w, row, g):
        along = []
        for q in range(n_chan):
            def at(i):
                return sky[row + RMAX + i, pl.ds(g, SUB), q * LANES : (q + 1) * LANES]
            value = w[0] * at(0)
            for k in range(1, RMAX + 1):
                value = value + w[k] * (at(-k) + at(k))
            along.append(value)
        return along

    def stencil(c):
        def one(j, carry):
            for u in range(8):
                jj = j * 8 + u
                row = c * STEP + jj // groups
                g = pl.multiple_of(lax.rem(jj, groups) * SUB, SUB)
                w = [taps[k, pl.ds(g, SUB), :] for k in range(RMAX + 1)]
                columns(w, rows_pass(w, row, g), g, row)
            return carry
        lax.fori_loop(0, STEP * groups // 8, one, 0)

    def chan_exchange(c):
        span = pl.ds(c * STEP, STEP)
        place = pl.ds(pl.multiple_of(chan * chans, chans), chans)
        for offset in CHAN_ORDER:
            peer = chan_peer(offset)
            pltpu.make_async_remote_copy(
                beam.at[peer, span], pencil.at[span, place], chan_send, chan_recv.at[c],
                device_id=(peer, tile), device_id_type=MESH,
            ).start()
        pltpu.make_async_copy(beam.at[chan, span], pencil.at[span, place], chan_recv.at[c]).start()

    def multiply(c):
        piece = pencil.at[pl.ds(c * STEP, STEP)]
        pltpu.make_async_copy(piece, piece, chan_recv.at[c]).wait()
        for pair in range(STEP // 2):
            row = c * STEP + 2 * pair
            value = jnp.concatenate([pencil[row], pencil[row + 1]], axis=1)
            parts = split(value)
            spectra = jnp.concatenate([parts[right] for _, right in PRODUCTS], axis=0)
            result = jnp.dot(matrix[...], spectra, preferred_element_type=F32)
            for half in range(2):
                outgoing[c, pl.ds(2 * pair + half, result.shape[0], stride=STEP), :] = result[
                    :, half * LANES : (half + 1) * LANES
                ]

    def tile_exchange(c):
        def source(owner):
            return outgoing.at[c, pl.ds(pl.multiple_of(owner * block, SUB), block)].reshape(CAP, STEP, LANES)
        for offset in TILE_ORDER:
            peer = tile_peer(offset)
            pltpu.make_async_remote_copy(
                source(peer), out_ref.at[:, tile, c], tile_send, tile_recv,
                device_id=(chan, peer), device_id_type=MESH,
            ).start()
        pltpu.make_async_copy(source(tile), out_ref.at[:, tile, c], tile_recv).start()

    def step(k, carry):
        @pl.when(k == steps - 2 * EDGE)
        def _():
            @pl.when(tile > 0)
            def _():
                up.wait_recv()

            @pl.when(tile < n_tile - 1)
            def _():
                down.wait_recv()

        @pl.when(k < steps)
        def _():
            @pl.when(k < steps - 3 * EDGE)
            def _():
                apply_mask(order(k) + EDGE)

            stencil(order(k))
            chan_exchange(order(k))

        @pl.when(k == 0)
        def _():
            lax.fori_loop(3 * EDGE, steps - EDGE, lambda c, carry: (load(c), carry)[1], 0)

        @pl.when(k == 1)
        def _():
            make_matrix(weight_ref, band_ref, resample_ref, slab_ref, matrix)

        @pl.when(k >= LEAD)
        def _():
            multiply(order(k - LEAD))
            tile_exchange(order(k - LEAD))
        return carry

    lax.fori_loop(0, steps + LEAD, step, 0)

    @pl.when(tile < n_tile - 1)
    def _():
        up.wait_send()

    @pl.when(tile > 0)
    def _():
        down.wait_send()

    sent = beam.at[pl.ds(0, n_chan - 1)]
    pltpu.make_async_copy(sent, sent, chan_send).wait()
    posted = outgoing.at[:, pl.ds(0, (n_tile - 1) * block)]
    pltpu.make_async_copy(posted, posted, tile_send).wait()
    pltpu.make_async_copy(out_ref, out_ref, tile_recv).wait()


def body(n_chan, n_tile, sky_cube, pixel_mask, radius, chan_weight, band, resample, slab_index):
    chans, rows, cols = sky_cube.shape
    steps = rows // STEP
    nch = n_chan * chans
    hbm = pl.BlockSpec(memory_space=pltpu.HBM)
    arrived = pl.pallas_call(
        kernel,
        out_shape=pltpu.VMEM((CAP, n_tile, steps, STEP, LANES), F32),
        in_specs=[hbm] * 7,
        out_specs=pl.BlockSpec(memory_space=pl.ANY),
        scratch_shapes=[
            pltpu.VMEM((rows, cols), jnp.int32),
            pltpu.VMEM((1, nch), jnp.int32),
            pltpu.VMEM((1, nch), F32),
            pltpu.VMEM(band.shape, F32),
            pltpu.VMEM(resample.shape, F32),
            pltpu.VMEM((1, slab_index.shape[0]), jnp.int32),
            pltpu.VMEM((rows + 2 * RMAX, chans, cols), F32),
            pltpu.VMEM((n_chan, rows, chans, LANES), F32),
            pltpu.VMEM((rows, nch, LANES), F32),
            pltpu.VMEM((steps, n_tile * CAP * STEP + SUB, LANES), F32),
            pltpu.VMEM((RMAX + 1, chans, LANES), F32),
            pltpu.VMEM((n_tile * CAP, len(PRODUCTS) * nch), BF16),
            pltpu.SemaphoreType.DMA((6,)),
            pltpu.SemaphoreType.DMA((steps,)),
            pltpu.SemaphoreType.DMA((2,)),
            pltpu.SemaphoreType.DMA((2,)),
            pltpu.SemaphoreType.DMA,
            pltpu.SemaphoreType.DMA((steps,)),
            pltpu.SemaphoreType.DMA,
            pltpu.SemaphoreType.DMA,
        ],
        compiler_params=pltpu.CompilerParams(
            collective_id=0, has_side_effects=True, vmem_limit_bytes=LIMIT
        ),
        name="slabs",
    )(
        *[
            pltpu.with_memory_space_constraint(x, pltpu.HBM)
            for x in (
                sky_cube, pixel_mask, radius[None, :], chan_weight[None, :], band, resample, slab_index[None, :]
            )
        ]
    )
    return arrived.reshape(CAP, n_tile * rows, LANES)


def solution(mesh):
    in_specs = (P("chan", "tile", None), P("tile", None), P(), P(), P(), P(), P())
    out_specs = P("tile", None, "chan")
    step = functools.partial(body, mesh.shape["chan"], mesh.shape["tile"])
    return jax.shard_map(step, mesh=mesh, in_specs=in_specs, out_specs=out_specs, check_vma=False)
```

```python
import functools

import jax
import jax.numpy as jnp
from jax import lax
from jax.experimental import pallas as pl
from jax.experimental.pallas import tpu as pltpu
from jax.sharding import PartitionSpec as P

MESH = pl.DeviceIdType.MESH
RMAX = 4
BW = 8
CAP = 20
LANES = 128
SUB = 8
STEP = 4
EDGE = RMAX // STEP
LEAD = 2
LIMIT = 50 * 2**20
TILE_ORDER = ((1,2),(2,1),(3,2),(2,3),(2,2),(1,1),(3,3),(1,3),(3,1),(2,0),(0,2),(1,0),(0,1),(3,0),(0,3))
CHAN_ORDER = ((1, 0), (3, 0), (2, 0), (1, 1), (3, 1), (2, 1), (0, 1))
F32 = jnp.float32
BF16 = jnp.bfloat16
PRODUCTS = ((0, 0), (0, 1), (1, 0))


def iota(shape, dim):
    return lax.broadcasted_iota(jnp.int32, shape, dim)


def split(value):
    parts = []
    for _ in range(2):
        part = value.astype(BF16)
        value = value - part.astype(F32)
        parts.append(part)
    return parts


def make_taps(radius_ref, taps_ref, first, chans):
    nch = radius_ref.shape[1]
    pick = iota((chans, nch), 1) == iota((chans, nch), 0) + first
    spread = jnp.sum(jnp.where(pick, radius_ref[...].astype(F32), 0.0), axis=1, keepdims=True)
    sigma = 0.5 * spread + 0.5
    values = []
    for k in range(RMAX + 1):
        value = jnp.exp(-float(k * k) / (2.0 * sigma * sigma))
        values.append(jnp.where(spread >= float(k), value, 0.0))
    total = values[0]
    for k in range(1, RMAX + 1):
        total = total + 2.0 * values[k]
    for k in range(RMAX + 1):
        taps_ref[k] = jnp.broadcast_to(values[k] / total, (chans, LANES))


def make_matrix(weight_ref, band_ref, resample_ref, slab_ref, matrix_ref):
    nch = weight_ref.shape[1]
    nout = resample_ref.shape[0]
    slots = matrix_ref.shape[0]
    distance = iota((nch, nch), 0) - iota((nch, nch), 1)
    filter_t = jnp.where(distance == 0, 1.0, 0.0)
    for o in range(2 * BW + 1):
        filter_t = filter_t - jnp.where(distance == o - BW, band_ref[o : o + 1, :], 0.0)
    combined = lax.dot_general(
        resample_ref[...], filter_t, (((1,), (1,)), ((), ())),
        precision=lax.Precision.HIGHEST, preferred_element_type=F32,
    ) * weight_ref[...]
    parts = split(combined)
    slab = slab_ref[...].astype(F32)
    eye = iota((nout, nout), 0) == iota((nout, nout), 1)
    slab_col = jnp.sum(jnp.where(eye, slab, 0.0), axis=1, keepdims=True)
    before = jnp.sum(jnp.where(slab_col < slab, 1.0, 0.0), axis=0, keepdims=True)
    rank = iota((1, nout), 1).astype(F32) - before
    code = slab * float(CAP) + rank
    chosen = jnp.where(iota((slots, nout), 0).astype(F32) == code, 1.0, 0.0).astype(BF16)
    picked = [jnp.dot(chosen, part, preferred_element_type=F32).astype(BF16) for part in parts]
    for i, (left, _) in enumerate(PRODUCTS):
        matrix_ref[:, i * nch : (i + 1) * nch] = picked[left]


def kernel(
    sky_ref, *rest
):
    small, rest = rest[:6], rest[6:]
    out_ref, rest = rest[0], rest[1:]
    (mask_ref, radius_ref, weight_ref, band_ref, resample_ref, slab_ref), rest = rest[:6], rest[6:]
    (
        sky, beam, pencil, outgoing, taps, matrix,
        small_sem, in_sem, halo_send, halo_recv, chan_send, chan_recv, tile_send, tile_recv,
    ) = rest
    local = (mask_ref, radius_ref, weight_ref, band_ref, resample_ref, slab_ref)
    fetches = [
        pltpu.make_async_copy(source, target, small_sem.at[i])
        for i, (source, target) in enumerate(zip(small, local))
    ]
    chan, tile = lax.axis_index("chan"), lax.axis_index("tile")
    n_chan, n_tile = beam.shape[0], out_ref.shape[1]
    chans, rows = sky_ref.shape[0], sky_ref.shape[1]
    nch = n_chan * chans
    steps = rows // STEP
    block = CAP * STEP

    def chan_peer(offset):
        dy, dc = offset
        return lax.rem(chan // 2 + dy, 4) * 2 + lax.rem(chan + dc, 2)

    def tile_peer(offset):
        dx, dz = offset
        return lax.rem(tile // 4 + dx, 4) * 4 + lax.rem(tile + dz, 4)

    def load(c):
        def one(i, carry):
            row = c * STEP + i
            pltpu.make_async_copy(sky_ref.at[:, row], sky.at[row + RMAX], in_sem.at[c]).start()
            return carry
        lax.fori_loop(0, STEP, one, 0)

    def order(k):
        return lax.rem(k + EDGE, steps)

    barrier = pltpu.get_barrier_semaphore()
    for offset in TILE_ORDER:
        pl.semaphore_signal(barrier, inc=1, device_id=(chan, tile_peer(offset)), device_id_type=MESH)
    for offset in CHAN_ORDER:
        pl.semaphore_signal(barrier, inc=1, device_id=(chan_peer(offset), tile), device_id_type=MESH)

    fetches[0].start()
    for c in range(EDGE):
        load(c)
        load(steps - 1 - c)
    for c in range(EDGE, 3 * EDGE):
        load(c)
    for fetch in fetches[1:]:
        fetch.start()

    def apply_mask(c):
        piece = sky.at[pl.ds(c * STEP + RMAX, STEP)]
        pltpu.make_async_copy(piece, piece, in_sem.at[c]).wait()

        def one(i, carry):
            row = c * STEP + i
            weight = mask_ref[pl.ds(row, 1), :].astype(F32)
            sky[row + RMAX] = sky[row + RMAX] * weight
            return carry
        lax.fori_loop(0, STEP, one, 0)

    @pl.when(tile == 0)
    def _():
        sky[0:RMAX] = jnp.zeros((RMAX,) + sky.shape[1:], F32)

    @pl.when(tile == n_tile - 1)
    def _():
        sky[rows + RMAX :] = jnp.zeros((RMAX,) + sky.shape[1:], F32)

    fetches[0].wait()
    for c in range(EDGE):
        apply_mask(c)
        apply_mask(steps - 1 - c)
    pl.semaphore_wait(barrier, len(CHAN_ORDER) + len(TILE_ORDER))

    up = pltpu.make_async_remote_copy(
        sky.at[pl.ds(rows, RMAX)], sky.at[pl.ds(0, RMAX)], halo_send.at[0], halo_recv.at[0],
        device_id=(chan, lax.rem(tile + 1, n_tile)), device_id_type=MESH,
    )
    down = pltpu.make_async_remote_copy(
        sky.at[pl.ds(RMAX, RMAX)], sky.at[pl.ds(rows + RMAX, RMAX)], halo_send.at[1], halo_recv.at[1],
        device_id=(chan, lax.rem(tile + n_tile - 1, n_tile)), device_id_type=MESH,
    )

    @pl.when(tile < n_tile - 1)
    def _():
        up.start()

    @pl.when(tile > 0)
    def _():
        down.start()

    for fetch in fetches[1:]:
        fetch.wait()
    make_taps(radius_ref, taps, chan * chans, chans)
    for c in range(EDGE, 2 * EDGE):
        apply_mask(c)

    groups = chans // SUB
    lane = iota((SUB, LANES), 1)

    def columns(w, along, g, row):
        zero = jnp.zeros((SUB, LANES), F32)
        last = len(along)
        ahead = [pltpu.roll(a, 1, 1) for a in along] + [zero]
        behind = [pltpu.roll(a, LANES - 1, 1) for a in along] + [zero]
        before = [jnp.where(lane < 1, ahead[q - 1], ahead[q]) for q in range(last + 1)]
        after = [jnp.where(lane >= LANES - 1, behind[(q + 1) % (last + 1)], behind[q]) for q in range(last + 1)]
        middle = [w[3] * a for a in along]
        upper = [w[2] * before[q] + (middle[q] + w[4] * after[q]) for q in range(last)] + [w[2] * before[last]]
        lower = [w[4] * before[q] + (middle[q] + w[2] * after[q]) for q in range(last)] + [w[2] * after[last]]
        upper = [pltpu.roll(a, LANES - 3, 1) for a in upper]
        lower = [pltpu.roll(a, 3, 1) for a in lower]
        for q in range(last):
            u = jnp.where(lane >= LANES - 3, upper[q + 1], upper[q])
            v = jnp.where(lane < 3, lower[q - 1], lower[q])
            beam[q, row, pl.ds(g, SUB), :] = (w[0] * along[q] + w[1] * (before[q] + after[q])) + (u + v)

    def rows_pass(w, row, g):
        along = []
        for q in range(n_chan):
            def at(i):
                return sky[row + RMAX + i, pl.ds(g, SUB), q * LANES : (q + 1) * LANES]
            value = w[0] * at(0)
            for k in range(1, RMAX + 1):
                value = value + w[k] * (at(-k) + at(k))
            along.append(value)
        return along

    def stencil(c):
        def one(j, carry):
            for u in range(8):
                jj = j * 8 + u
                row = c * STEP + jj // groups
                g = pl.multiple_of(lax.rem(jj, groups) * SUB, SUB)
                w = [taps[k, pl.ds(g, SUB), :] for k in range(RMAX + 1)]
                columns(w, rows_pass(w, row, g), g, row)
            return carry
        lax.fori_loop(0, STEP * groups // 8, one, 0)

    def chan_exchange(c):
        span = pl.ds(c * STEP, STEP)
        place = pl.ds(pl.multiple_of(chan * chans, chans), chans)
        for offset in CHAN_ORDER:
            peer = chan_peer(offset)
            pltpu.make_async_remote_copy(
                beam.at[peer, span], pencil.at[span, place], chan_send, chan_recv.at[c],
                device_id=(peer, tile), device_id_type=MESH,
            ).start()
        pltpu.make_async_copy(beam.at[chan, span], pencil.at[span, place], chan_recv.at[c]).start()

    def multiply(c):
        piece = pencil.at[pl.ds(c * STEP, STEP)]
        pltpu.make_async_copy(piece, piece, chan_recv.at[c]).wait()
        for pair in range(STEP // 2):
            row = c * STEP + 2 * pair
            value = jnp.concatenate([pencil[row], pencil[row + 1]], axis=1)
            parts = split(value)
            spectra = jnp.concatenate([parts[right] for _, right in PRODUCTS], axis=0)
            result = jnp.dot(matrix[...], spectra, preferred_element_type=F32)
            for half in range(2):
                outgoing[c, pl.ds(2 * pair + half, result.shape[0], stride=STEP), :] = result[
                    :, half * LANES : (half + 1) * LANES
                ]

    def tile_exchange(c):
        def source(owner):
            return outgoing.at[c, pl.ds(pl.multiple_of(owner * block, SUB), block)].reshape(CAP, STEP, LANES)
        for offset in TILE_ORDER:
            peer = tile_peer(offset)
            pltpu.make_async_remote_copy(
                source(peer), out_ref.at[:, tile, c], tile_send, tile_recv,
                device_id=(chan, peer), device_id_type=MESH,
            ).start()
        pltpu.make_async_copy(source(tile), out_ref.at[:, tile, c], tile_recv).start()

    def step(k, carry):
        @pl.when(k == steps - 2 * EDGE)
        def _():
            @pl.when(tile > 0)
            def _():
                up.wait_recv()

            @pl.when(tile < n_tile - 1)
            def _():
                down.wait_recv()

        @pl.when(k < steps)
        def _():
            @pl.when(k < steps - 3 * EDGE)
            def _():
                apply_mask(order(k) + EDGE)

            stencil(order(k))
            chan_exchange(order(k))

        @pl.when(k == 0)
        def _():
            lax.fori_loop(3 * EDGE, steps - EDGE, lambda c, carry: (load(c), carry)[1], 0)

        @pl.when(k == 1)
        def _():
            make_matrix(weight_ref, band_ref, resample_ref, slab_ref, matrix)

        @pl.when(k >= LEAD)
        def _():
            multiply(order(k - LEAD))
            tile_exchange(order(k - LEAD))
        return carry

    lax.fori_loop(0, steps + LEAD, step, 0)

    @pl.when(tile < n_tile - 1)
    def _():
        up.wait_send()

    @pl.when(tile > 0)
    def _():
        down.wait_send()

    sent = beam.at[pl.ds(0, n_chan - 1)]
    pltpu.make_async_copy(sent, sent, chan_send).wait()
    posted = outgoing.at[:, pl.ds(0, (n_tile - 1) * block)]
    pltpu.make_async_copy(posted, posted, tile_send).wait()
    pltpu.make_async_copy(out_ref, out_ref, tile_recv).wait()


def body(n_chan, n_tile, sky_cube, pixel_mask, radius, chan_weight, band, resample, slab_index):
    chans, rows, cols = sky_cube.shape
    steps = rows // STEP
    nch = n_chan * chans
    hbm = pl.BlockSpec(memory_space=pltpu.HBM)
    arrived = pl.pallas_call(
        kernel,
        out_shape=pltpu.VMEM((CAP, n_tile, steps, STEP, LANES), F32),
        in_specs=[hbm] * 7,
        out_specs=pl.BlockSpec(memory_space=pl.ANY),
        scratch_shapes=[
            pltpu.VMEM((rows, cols), jnp.int32),
            pltpu.VMEM((1, nch), jnp.int32),
            pltpu.VMEM((1, nch), F32),
            pltpu.VMEM(band.shape, F32),
            pltpu.VMEM(resample.shape, F32),
            pltpu.VMEM((1, slab_index.shape[0]), jnp.int32),
            pltpu.VMEM((rows + 2 * RMAX, chans, cols), F32),
            pltpu.VMEM((n_chan, rows, chans, LANES), F32),
            pltpu.VMEM((rows, nch, LANES), F32),
            pltpu.VMEM((steps, n_tile * CAP * STEP + SUB, LANES), F32),
            pltpu.VMEM((RMAX + 1, chans, LANES), F32),
            pltpu.VMEM((n_tile * CAP, len(PRODUCTS) * nch), BF16),
            pltpu.SemaphoreType.DMA((6,)),
            pltpu.SemaphoreType.DMA((steps,)),
            pltpu.SemaphoreType.DMA((2,)),
            pltpu.SemaphoreType.DMA((2,)),
            pltpu.SemaphoreType.DMA,
            pltpu.SemaphoreType.DMA((steps,)),
            pltpu.SemaphoreType.DMA,
            pltpu.SemaphoreType.DMA,
        ],
        compiler_params=pltpu.CompilerParams(
            collective_id=0, has_side_effects=True, vmem_limit_bytes=LIMIT
        ),
        name="slabs",
    )(
        *[
            pltpu.with_memory_space_constraint(x, pltpu.HBM)
            for x in (
                sky_cube, pixel_mask, radius[None, :], chan_weight[None, :], band, resample, slab_index[None, :]
            )
        ]
    )
    return arrived.reshape(CAP, n_tile * rows, LANES)


def solution(mesh):
    in_specs = (P("chan", "tile", None), P("tile", None), P(), P(), P(), P(), P())
    out_specs = P("tile", None, "chan")
    step = functools.partial(body, mesh.shape["chan"], mesh.shape["tile"])
    return jax.shard_map(step, mesh=mesh, in_specs=in_specs, out_specs=out_specs, check_vma=False)
```
